32 devices in a mesh: user: 4 (over z), item: 8 (over y, x, core).
Axes of the slice: x: 2, y: 2, z: 4, core: 2. Of those that a mesh axis runs over, the one named last changes fastest.
Arguments:
- values: bfloat16 [4, 8, 256, 128], P('user', 'item'), may hold values from -6 to 6
- block_user: int32 [4, 8, 256], P('user', 'item'), may hold values from 0 to 63
- block_item: int32 [4, 8, 256], P('user', 'item'), may hold values from 0 to 2047
- block_ctx: int32 [4, 8, 256], P('user', 'item'), may hold values from 0 to 128
- block_count: int32 [4, 8], P('user', 'item'), may hold values from 64 to 256, as said below
- core: bfloat16 [32, 32, 32], replicated, may hold values from -1 to 1
- item_factor: bfloat16 [16384, 32], P(('item', 'user')), may hold values from -6 to 6
- ctx_factor: bfloat16 [256, 32], replicated, may hold values from -0.03125 to 0.03125
Outputs:
- user_factor: float32 [256, 32], P('user')
The draws below stay inside these ranges and needn't reach their ends.
Inputs may be any that keep to these rules, and one draw needn't show every extreme that they name: A tile's live slots are its first block_count slots; some tile has all 256 slots live in every draw.
All inputs are finite; a program needn't handle non-finite values.
Results may differ from the reference program's by a relative error of at most 0.0047.
Values may be sent and summed in bfloat16 or wider, within the bound.
A program may use at most 64 MiB of HBM per device.

```python
import math
import jax
import jax.numpy as jnp
import numpy as np
from jax import lax

RANK = 32
CTX = 256
BW = 128
U_SH = 64
I_SH = 2048
CAP = 256
USERS = 256
ITEMS = 16384
N_USER = 4
N_ITEM = 8


def draw_block_count(key, part):
    drawn = jax.random.randint(key, (N_USER, N_ITEM), CAP // 4, CAP + 1)
    chosen = jax.random.randint(jax.random.fold_in(key, 7), (), 0, N_USER * N_ITEM)
    places = jnp.arange(N_USER * N_ITEM, dtype=jnp.int32).reshape(N_USER, N_ITEM)
    return jnp.where(places == chosen, CAP, drawn).astype(jnp.int32)


def touch_ends(entries, own_key, least, largest):
    longest = entries.shape.index(max(entries.shape))
    spots = []
    for shift in (0, 1):
        where = [jax.random.randint(jax.random.fold_in(own_key, axis), (), 0, length) for axis, length in enumerate(entries.shape)]
        where[longest] = (where[longest] + shift) % entries.shape[longest]
        spots.append(tuple(where))
    return entries.at[spots[0]].set(least).at[spots[1]].set(largest)


def steps_of(key, extent, pieces, low, high):
    loudness, own = 1.0, jax.random.fold_in(key, 6)
    for dim, blocks in pieces:
        draws = jnp.exp(jax.random.uniform(jax.random.fold_in(own, dim), (blocks,), jnp.float32, low / len(pieces), high / len(pieces)))
        loudness = loudness * jnp.repeat(draws, extent[dim] // blocks).reshape([-1 if axis == dim else 1 for axis in range(len(extent))])
    return loudness


def rank_table(number_of, slope):
    weights = [(1 << 20) // math.isqrt(standing ** slope) + 1 for standing in range(1, number_of + 1)]
    spread = 1 + sum(weights) // (1 << 30)
    return np.cumsum(np.array([max(1, weight // spread) for weight in weights]))


def ranked(rng, dims, amount, slope):
    grid = rank_table(amount, slope)
    ticket = jax.random.randint(jax.random.fold_in(rng, 1), dims, 0, int(grid[amount - 1]))
    standing = jnp.searchsorted(jnp.asarray(grid, jnp.int32), ticket, side="right")
    return jax.random.permutation(jax.random.fold_in(rng, 2), amount)[standing].astype(jnp.int32)


def centred(stream_key, dims, scale, bound, pieces=(), held_as=jnp.bfloat16):
    level = steps_of(stream_key, dims, pieces, -0.22, 0.18) if pieces else 1.0
    result = jax.random.normal(stream_key, dims, jnp.float32) * scale * level
    return jnp.minimum(jnp.maximum(result, -bound), bound).astype(held_as)


def setup_inputs(seed: int = 0) -> dict:
    key_of = jax.random.split(jax.random.key(seed), 9)
    return {
        "values": centred(key_of[0], (N_USER, N_ITEM, CAP, BW), 1.0, 6.0, ((0, 4), (1, 8))),
        "block_user": touch_ends(ranked(key_of[1], (N_USER, N_ITEM, CAP), U_SH, 2), jax.random.fold_in(key_of[1], 3), 0, U_SH - 1).astype(jnp.int32),
        "block_item": touch_ends(jax.random.randint(key_of[2], (N_USER, N_ITEM, CAP), 0, I_SH), jax.random.fold_in(key_of[2], 1), 0, I_SH - 1).astype(jnp.int32),
        "block_ctx": touch_ends(jax.random.randint(key_of[3], (N_USER, N_ITEM, CAP), 0, CTX - BW + 1), jax.random.fold_in(key_of[3], 1), 0, CTX - BW).astype(jnp.int32),
        "block_count": draw_block_count(jax.random.fold_in(key_of[8], 71), 0),
        "core": centred(key_of[5], (RANK, RANK, RANK), RANK ** -0.5, 1.0),
        "item_factor": centred(key_of[6], (ITEMS, RANK), 1.0, 6.0, ((0, 32),)),
        "ctx_factor": centred(key_of[7], (CTX, RANK), (RANK * 1024) ** -0.5, 0.03125),
    }


ridge = 0.1

def tile_terms(slab_vals, user_ids, item_ids, ctx_starts, live_count, proj_tile, ctx_factor):
    slots = slab_vals.shape[0]
    offsets = ctx_starts[:, None] + jnp.arange(BW, dtype=jnp.int32)[None, :]
    window = ctx_factor[offsets].astype(jnp.float32)
    chosen = proj_tile[item_ids].astype(jnp.float32)
    feature = jnp.einsum('bak,bck->bac', chosen, window).astype(jnp.bfloat16).astype(jnp.float32)
    live = (jnp.arange(slots, dtype=jnp.int32) < live_count).astype(jnp.float32)
    grams = jnp.einsum('bac,bdc->bad', feature, feature) * live[:, None, None]
    target = jnp.einsum('bac,bc->ba', feature, slab_vals.astype(jnp.float32)) * live[:, None]
    normal = jax.ops.segment_sum(grams.reshape(slots, RANK * RANK), user_ids, U_SH)
    return (normal, jax.ops.segment_sum(target, user_ids, U_SH))

def reference(values, block_user, block_item, block_ctx, block_count, core, item_factor, ctx_factor):
    proj = jnp.einsum('ib,abk->iak', item_factor.astype(jnp.float32), core.astype(jnp.float32)).astype(jnp.bfloat16)
    proj = proj.reshape(N_ITEM, I_SH, RANK, RANK)

    def user_shard(index):

        def add(carry, column):
            normal, target = tile_terms(values[index, column], block_user[index, column], block_item[index, column], block_ctx[index, column], block_count[index, column], proj[column], ctx_factor)
            return ((carry[0] + normal, carry[1] + target), None)
        start = (jnp.zeros((U_SH, RANK * RANK), jnp.float32), jnp.zeros((U_SH, RANK), jnp.float32))
        (normal, target), _ = lax.scan(add, start, jnp.arange(N_ITEM, dtype=jnp.int32))
        matrix = normal.reshape(U_SH, RANK, RANK) + ridge * jnp.eye(RANK, dtype=jnp.float32)
        return jnp.linalg.solve(matrix, target[..., None])[..., 0]
    solved = lax.map(user_shard, jnp.arange(N_USER, dtype=jnp.int32))
    return solved.reshape(USERS, RANK)
```

```python
import functools

import jax
import jax.numpy as jnp
from jax import lax
from jax.experimental import pallas as pl
from jax.experimental.pallas import tpu as pltpu
from jax.sharding import PartitionSpec as P

U_SH = 64
RIDGE = 0.1
MESH = pl.DeviceIdType.MESH
F32 = jnp.float32
BF16 = jnp.bfloat16
NT = (((1,), (1,)), ((), ()))


def iota(shape, dim):
    return lax.broadcasted_iota(jnp.int32, shape, dim)


def lanes_of(x, index):
    return jnp.take_along_axis(x, index, axis=1, mode="promise_in_bounds")


def solve(mats, target):
    shape = mats[0].shape
    lane = iota(shape, 1)
    block, place = lane >> 5, lane & 31
    count = len(mats)
    mats = [m + jnp.where(place == 4 * j + block, RIDGE, 0.0) for j, m in enumerate(mats)]
    cols = [lanes_of(target, 4 * j + block) for j in range(count)]
    for k in range(4 * count):
        jk, ck = divmod(k, 4)
        pivot = lanes_of(mats[jk], jnp.full(shape, ck * 32 + k, jnp.int32))
        row = lanes_of(mats[jk], ck * 32 + place)
        rhs = lanes_of(cols[jk], ck * 32 + place)
        factor = [lanes_of(m, (block << 5) + k) for m in mats]
        factor[jk] = jnp.where(block == ck, 0.0, factor[jk])
        inverse = 1.0 / pivot
        row, rhs = row * inverse, rhs * inverse
        mats = [m - f * row for m, f in zip(mats, factor)]
        cols = [c - f * rhs for c, f in zip(cols, factor)]
    answer = jnp.zeros(shape, F32)
    for j in range(count):
        x = cols[j] / lanes_of(mats[j], (block << 5) + 4 * j + block)
        answer = jnp.where((lane >> 2) == j, lanes_of(x, (lane & 3) << 5), answer)
    return answer


def kernel(
    n_user, n_item,
    values, b_user, b_item, b_ctx, b_count, core, item, ctx, out,
    fac, starts, bt, yb, rf, gb, pay, recv, xg,
    fac_send, fac_recv, pay_send, pay_recv, x_send, x_recv,
):
    me_u, me_i = lax.axis_index("user"), lax.axis_index("item")
    slots, bw = values.shape[2], values.shape[3]
    rank = core.shape[0]
    rows = item.shape[0]
    quarter = rows // 4
    packs = rank // 4
    per = U_SH // n_item

    barrier = pltpu.get_barrier_semaphore()
    for d in range(1, n_user):
        pl.semaphore_signal(barrier, inc=1, device_id={"user": lax.rem(me_u + d, n_user)}, device_id_type=MESH)
    for d in range(1, n_item):
        pl.semaphore_signal(barrier, inc=1, device_id={"item": lax.rem(me_i + d, n_item)}, device_id_type=MESH)

    own = item[...].astype(F32)
    fac[0] = jnp.concatenate([own[c * quarter : (c + 1) * quarter] for c in range(4)], axis=1).astype(BF16)
    pl.semaphore_wait(barrier, n_user + n_item - 2)
    fac_copies = []
    for d in range(1, n_user):
        copy = pltpu.make_async_remote_copy(
            src_ref=fac.at[0], dst_ref=fac.at[d], send_sem=fac_send.at[d], recv_sem=fac_recv.at[d],
            device_id={"user": lax.rem(me_u + d, n_user)}, device_id_type=MESH,
        )
        copy.start()
        fac_copies.append(copy)

    ids = b_item[0]
    starts_row = b_ctx[0]
    parts = [jnp.broadcast_to(r.astype(F32), (128, slots)) for r in (starts_row, ids >> 7, ids & 127)]
    eye = (iota((slots, slots), 0) == iota((slots, slots), 1)).astype(F32).astype(BF16)
    columns = lax.dot_general(eye, jnp.concatenate(parts, axis=0).astype(BF16), NT, preferred_element_type=F32)
    start_col = columns[:, :128].astype(jnp.int32)
    item_col = (columns[:, 128:256] * 128.0 + columns[:, 256:384]).astype(jnp.int32)
    starts[...] = start_col

    turned = values[0, 0].astype(F32)
    for bit in range(bw.bit_length() - 1):
        turned = jnp.where(((start_col >> bit) & 1) == 1, pltpu.roll(turned, 1 << bit, 1), turned)
    rf[pl.ds(rank * slots, slots), :] = turned
    rf[pl.ds((rank + 1) * slots, slots), :] = jnp.zeros((slots, bw), F32)

    cores = core[...].astype(F32)
    mixing = jnp.concatenate([cores[a] for a in range(rank)], axis=1)
    mixing = jnp.concatenate([mixing] * 4, axis=0).astype(BF16)
    ctx_rows = jnp.concatenate([ctx[...].astype(F32)] * 4, axis=1)
    ctx_block = iota(ctx_rows.shape, 1) >> 5
    for c in range(4):
        bt[c] = jnp.where(ctx_block == c, ctx_rows, 0.0).astype(BF16)
    live = iota((U_SH, slots), 1) < b_count[...]
    onehot = jnp.where((iota((U_SH, slots), 0) == b_user[0]) & live, 1.0, 0.0).astype(BF16)

    wide = n_user * quarter
    lane = iota((slots, wide), 1)
    owner = (me_u - (lane >> (quarter.bit_length() - 1)) + n_user) & (n_user - 1)
    held = owner * rows + (lane & (quarter - 1))
    wanted = jnp.concatenate([item_col] * (wide // 128), axis=1)
    picks = [jnp.where(held + c * quarter == wanted, 1.0, 0.0).astype(BF16) for c in range(4)]

    for copy in fac_copies:
        copy.wait()
    table = fac[...].reshape(wide, 128)
    slot_block = iota((slots, 128), 1) >> 5
    chosen = jnp.zeros((slots, 128), F32)
    for c in range(4):
        got = jnp.dot(picks[c], table, preferred_element_type=F32)
        chosen = jnp.where(slot_block == c, got, chosen)
    proj = jnp.dot(chosen.astype(BF16), mixing, preferred_element_type=F32).astype(BF16)
    for j in range(packs):
        yb[j] = proj[:, 128 * j : 128 * (j + 1)]

    def features(j, carry):
        first = iota((slots, bw), 1) >= starts[...]
        z = yb[j]
        for c in range(4):
            full = lax.dot_general(z, bt[c], NT, preferred_element_type=F32)
            rf[pl.ds(pl.multiple_of((4 * j + c) * slots, slots), slots), :] = jnp.where(first, full[:, :bw], full[:, bw:])
        return carry

    lax.fori_loop(0, packs, features, 0)

    def grams(g, carry):
        base = pl.multiple_of(8 * g, 8)
        left = jnp.concatenate([rf[pl.ds(a * slots + base, 8), :] for a in range(rank + 2)], axis=0).astype(BF16)
        right = jnp.concatenate([rf[pl.ds(base + s, rank, stride=slots), :] for s in range(8)], axis=0).astype(BF16)
        full = lax.dot_general(left, right, NT, preferred_element_type=F32)
        sub, ln = iota((8, 128), 0), iota((8, 128), 1)
        low, same = sub < 4, (ln >> 5) == (sub & 3)
        for a in range(rank + 1):
            part = full[8 * a : 8 * a + 8]
            gb[pl.ds(a * slots + base, 8), :] = jnp.where(same, jnp.where(low, part[:, :128], part[:, 128:]), 0.0)
        return carry

    lax.fori_loop(0, slots // 8, grams, 0)

    def summed(a):
        x = gb[pl.ds(pl.multiple_of(a * slots, slots), slots), :]
        high = x.astype(BF16)
        rest = (x - high.astype(F32)).astype(BF16)
        both = jnp.dot(onehot, jnp.concatenate([high, rest], axis=1), preferred_element_type=F32)
        return both[:, :128] + both[:, 128:]

    if per < 8:
        pay[...] = jnp.zeros(pay.shape, F32)

    def put(j, x):
        for q in range(n_item):
            pay[q, j, 0:per, :] = x[q * per : (q + 1) * per]

    def segments(j, carry):
        blk = iota((U_SH, 128), 1) >> 5
        x, w, y, v = (summed(4 * j + c) for c in range(4))
        low, mid, even = blk < 2, (blk == 1) | (blk == 2), (blk & 1) == 0
        one = jnp.where(low, x, y) + pltpu.roll(jnp.where(low, y, x), 64, 1)
        two = jnp.where(mid, w, v) + pltpu.roll(jnp.where(mid, v, w), 64, 1)
        put(j, jnp.where(even, one, two) + pltpu.roll(jnp.where(even, two, one), 96, 1))
        return carry

    lax.fori_loop(0, packs, segments, 0)
    aim = summed(rank)
    aim = aim + pltpu.roll(aim, 64, 1)
    put(packs, aim + pltpu.roll(aim, 32, 1))

    pay_copies = []
    for d in range(1, n_item):
        to = lax.rem(me_i + d, n_item)
        copy = pltpu.make_async_remote_copy(
            src_ref=pay.at[to], dst_ref=recv.at[d], send_sem=pay_send.at[d], recv_sem=pay_recv.at[d],
            device_id={"item": to}, device_id_type=MESH,
        )
        copy.start()
        pay_copies.append(copy)
    for copy in pay_copies:
        copy.wait()
    total = pay[me_i]
    for d in range(1, n_item):
        total = total + recv[d]
    answer = solve([total[j] for j in range(packs)], total[packs])

    xg[me_i] = answer
    x_copies = []
    for d in range(1, n_item):
        copy = pltpu.make_async_remote_copy(
            src_ref=xg.at[me_i], dst_ref=xg.at[me_i], send_sem=x_send.at[d], recv_sem=x_recv.at[d],
            device_id={"item": lax.rem(me_i + d, n_item)}, device_id_type=MESH,
        )
        copy.start()
        x_copies.append(copy)
    for d in range(1, n_item):
        x_copies[d - 1].wait_send()
        source = lax.rem(me_i + n_item - d, n_item)
        pltpu.make_async_remote_copy(
            src_ref=xg.at[source], dst_ref=xg.at[source], send_sem=x_send.at[d], recv_sem=x_recv.at[d],
            device_id={"item": lax.rem(me_i + d, n_item)}, device_id_type=MESH,
        ).wait_recv()
    for q in range(n_item):
        out[q * per : (q + 1) * per, :] = xg[q, 0:per, 0:rank]


def solution(mesh):
    n_user, n_item = mesh.shape["user"], mesh.shape["item"]
    placed = (
        P("user", "item", None, None),
        P("user", "item", None),
        P("user", "item", None),
        P("user", "item", None),
        P("user", "item"),
        P(),
        P(("item", "user"), None),
        P(),
    )

    def local(values, block_user, block_item, block_ctx, block_count, core, item_factor, ctx_factor):
        rank = core.shape[0]
        slots, bw = values.shape[2], values.shape[3]
        quarter = item_factor.shape[0] // 4
        packs = rank // 4
        return pl.pallas_call(
            functools.partial(kernel, n_user, n_item),
            out_shape=jax.ShapeDtypeStruct((U_SH, rank), F32),
            in_specs=[pl.BlockSpec(memory_space=pltpu.VMEM)] * 8,
            out_specs=pl.BlockSpec(memory_space=pltpu.VMEM),
            scratch_shapes=[
                pltpu.VMEM((n_user, quarter, 128), BF16),
                pltpu.VMEM((slots, 128), jnp.int32),
                pltpu.VMEM((4, ctx_factor.shape[0], 128), BF16),
                pltpu.VMEM((packs, slots, 128), BF16),
                pltpu.VMEM(((rank + 2) * slots, bw), F32),
                pltpu.VMEM(((rank + 1) * slots, 128), F32),
                pltpu.VMEM((n_item, packs + 1, 8, 128), F32),
                pltpu.VMEM((n_item, packs + 1, 8, 128), F32),
                pltpu.VMEM((n_item, 8, 128), F32),
                pltpu.SemaphoreType.DMA((n_user,)),
                pltpu.SemaphoreType.DMA((n_user,)),
                pltpu.SemaphoreType.DMA((n_item,)),
                pltpu.SemaphoreType.DMA((n_item,)),
                pltpu.SemaphoreType.DMA((n_item,)),
                pltpu.SemaphoreType.DMA((n_item,)),
            ],
            compiler_params=pltpu.CompilerParams(
                collective_id=0, has_side_effects=True, vmem_limit_bytes=40 * 1024 * 1024
            ),
        )(values, block_user, block_item, block_ctx, block_count, core, item_factor, ctx_factor)

    return jax.shard_map(local, mesh=mesh, in_specs=placed, out_specs=P("user", None), check_vma=False)
```

```python
import functools

import jax
import jax.numpy as jnp
from jax import lax
from jax.experimental import pallas as pl
from jax.experimental.pallas import tpu as pltpu
from jax.sharding import PartitionSpec as P

U_SH = 64
RIDGE = 0.1
MESH = pl.DeviceIdType.MESH
F32 = jnp.float32
BF16 = jnp.bfloat16
NT = (((1,), (1,)), ((), ()))


def iota(shape, dim):
    return lax.broadcasted_iota(jnp.int32, shape, dim)


def lanes_of(x, index):
    return jnp.take_along_axis(x, index, axis=1, mode="promise_in_bounds")


def solve(mats, target):
    shape = mats[0].shape
    lane = iota(shape, 1)
    block, place = lane >> 5, lane & 31
    count = len(mats)
    mats = [m + jnp.where(place == 4 * j + block, RIDGE, 0.0) for j, m in enumerate(mats)]
    cols = [lanes_of(target, 4 * j + block) for j in range(count)]
    own = [jnp.zeros(shape, F32)] * count
    off = [jnp.zeros(shape, F32)] * count
    for k in range(0, 4 * count, 2):
        jk, ck = divmod(k, 4)
        pair = mats[jk]
        p, s, q = (lanes_of(pair, jnp.full(shape, i, jnp.int32)) for i in (ck * 32 + k, ck * 32 + k + 1, ck * 32 + 33 + k))
        row0, row1 = (lanes_of(pair, (ck + i) * 32 + place) for i in (0, 1))
        rhs0, rhs1 = (lanes_of(cols[jk], (ck + i) * 32 + place) for i in (0, 1))
        factor0 = [lanes_of(m, (block << 5) + k) for m in mats]
        factor1 = [lanes_of(m, (block << 5) + k + 1) for m in mats]
        here = (block >> 1) == ck // 2
        factor0[jk], factor1[jk] = jnp.where(here, 0.0, factor0[jk]), jnp.where(here, 0.0, factor1[jk])
        inverse = 1.0 / (p * q - s * s)
        p, s, q = p * inverse, s * inverse, q * inverse
        own[jk] = jnp.where(here, jnp.where((block & 1) == 0, q, p), own[jk])
        off[jk] = jnp.where(here, s, off[jk])
        row0, row1 = q * row0 - s * row1, p * row1 - s * row0
        rhs0, rhs1 = q * rhs0 - s * rhs1, p * rhs1 - s * rhs0
        mats = [m - (f0 * row0 + f1 * row1) for m, f0, f1 in zip(mats, factor0, factor1)]
        cols = [c - (f0 * rhs0 + f1 * rhs1) for c, f0, f1 in zip(cols, factor0, factor1)]
    answer = jnp.zeros(shape, F32)
    for j in range(count):
        x = own[j] * cols[j] - off[j] * lanes_of(cols[j], (block ^ 1) << 5)
        answer = jnp.where((lane >> 2) == j, lanes_of(x, (lane & 3) << 5), answer)
    return answer


def kernel(
    n_user, n_item,
    values_hbm, user_hbm, item_hbm, ctx_hbm, count_hbm, core_hbm, rows_hbm, slab_hbm, out,
    values, b_user, b_item, b_ctx, b_count, core, slab,
    fac, starts, bt, yb, rf, gb, pay, recv, xg,
    load, fac_send, fac_recv, pay_send, pay_recv, x_send, x_recv,
):
    me_u, me_i = lax.axis_index("user"), lax.axis_index("item")
    slots, bw = values.shape
    rank = core.shape[0]
    rows = rows_hbm.shape[1]
    packs = rank // 4
    per = U_SH // n_item

    barrier = pltpu.get_barrier_semaphore()
    for d in range(1, n_user):
        pl.semaphore_signal(barrier, inc=1, device_id={"user": lax.rem(me_u + d, n_user)}, device_id_type=MESH)
    for d in range(1, n_item):
        pl.semaphore_signal(barrier, inc=1, device_id={"item": lax.rem(me_i + d, n_item)}, device_id_type=MESH)

    loads = [
        pltpu.make_async_copy(source, target, load.at[i])
        for i, (source, target) in enumerate((
            (ctx_hbm.at[0], b_ctx), (item_hbm.at[0], b_item), (user_hbm.at[0], b_user), (count_hbm, b_count),
            (values_hbm.at[0, 0], values), (rows_hbm, fac.at[0]), (core_hbm, core), (slab_hbm, slab),
        ))
    ]
    for copy in loads:
        copy.start()
    pl.semaphore_wait(barrier, n_user + n_item - 2)
    fac_copies = []
    for d in range(1, n_user):
        copy = pltpu.make_async_remote_copy(
            src_ref=rows_hbm, dst_ref=fac.at[d], send_sem=fac_send.at[d], recv_sem=fac_recv.at[d],
            device_id={"user": lax.rem(me_u + d, n_user)}, device_id_type=MESH,
        )
        copy.start()
        fac_copies.append(copy)
    for copy in loads:
        copy.wait()

    ids = b_item[...]
    parts = [jnp.broadcast_to(r.astype(F32), (128, slots)) for r in (b_ctx[...], ids >> 7, ids & 127)]
    eye = (iota((slots, slots), 0) == iota((slots, slots), 1)).astype(F32).astype(BF16)
    columns = lax.dot_general(eye, jnp.concatenate(parts, axis=0).astype(BF16), NT, preferred_element_type=F32)
    start_col = columns[:, :128].astype(jnp.int32)
    item_col = (columns[:, 128:256] * 128.0 + columns[:, 256:384]).astype(jnp.int32)
    starts[...] = start_col

    turned = values[...].astype(F32)
    for bit in range(bw.bit_length() - 1):
        turned = jnp.where(((start_col >> bit) & 1) == 1, pltpu.roll(turned, 1 << bit, 1), turned)
    rf[pl.ds(rank * slots, slots), :] = turned
    rf[pl.ds((rank + 1) * slots, slots), :] = jnp.zeros((slots, bw), F32)

    cores = core[...].astype(F32)
    mixing = jnp.concatenate([cores[a] for a in range(rank)], axis=1).astype(BF16)
    for c in range(4):
        pieces = [jnp.zeros(slab.shape, BF16)] * 4
        pieces[c] = slab[...]
        bt[c] = jnp.concatenate(pieces, axis=0)
    live = iota((U_SH, slots), 1) < b_count[...]
    onehot = jnp.where((iota((U_SH, slots), 0) == b_user[...]) & live, 1.0, 0.0).astype(BF16)

    wanted = jnp.concatenate([item_col] * (rows // 128), axis=1)
    lane = iota((slots, rows), 1)
    chosen = jnp.zeros((slots, rank), F32)
    for d in range(n_user):
        held = lax.rem(me_u + n_user - d, n_user) * rows
        picks = jnp.where(lane + held == wanted, 1.0, 0.0).astype(BF16)
        if d:
            fac_copies[d - 1].wait()
        chosen = chosen + lax.dot_general(picks, fac[d], NT, preferred_element_type=F32)
    proj = jnp.dot(chosen.astype(BF16), mixing, preferred_element_type=F32).astype(BF16)
    for j in range(packs):
        yb[j] = proj[:, 128 * j : 128 * (j + 1)]

    def features(j, carry):
        first = iota((slots, bw), 1) >= starts[...]
        z = yb[j]
        for c in range(4):
            full = jnp.dot(z, bt[c], preferred_element_type=F32)
            rf[pl.ds(pl.multiple_of((4 * j + c) * slots, slots), slots), :] = jnp.where(first, full[:, :bw], full[:, bw:])
        return carry

    lax.fori_loop(0, packs, features, 0)

    unrolled = 4

    def grams(turn, carry):
        sub, ln = iota((8, 128), 0), iota((8, 128), 1)
        low, same = sub < 4, (ln >> 5) == (sub & 3)
        bases = [pl.multiple_of(8 * (unrolled * turn + i), 8) for i in range(unrolled)]
        kept = []
        for base in bases:
            left = jnp.concatenate([rf[pl.ds(a * slots + base, 8), :] for a in range(rank + 2)], axis=0).astype(BF16)
            right = jnp.concatenate([rf[pl.ds(base + s, rank, stride=slots), :] for s in range(8)], axis=0).astype(BF16)
            kept.append(lax.dot_general(left, right, NT, preferred_element_type=F32))
        for base, full in zip(bases, kept):
            for a in range(rank + 1):
                part = full[8 * a : 8 * a + 8]
                gb[pl.ds(a * slots + base, 8), :] = jnp.where(same, jnp.where(low, part[:, :128], part[:, 128:]), 0.0)
        return carry

    lax.fori_loop(0, slots // (8 * unrolled), grams, 0)

    def summed(a):
        x = gb[pl.ds(a * slots, slots), :]
        high = x.astype(BF16)
        rest = (x - high.astype(F32)).astype(BF16)
        both = jnp.dot(onehot, jnp.concatenate([high, rest], axis=1), preferred_element_type=F32)
        return both[:, :128] + both[:, 128:]

    if per < 8:
        pay[...] = jnp.zeros(pay.shape, F32)

    def put(j, x):
        for q in range(n_item):
            pay[q, j, 0:per, :] = x[q * per : (q + 1) * per]

    blk = iota((U_SH, 128), 1) >> 5
    low, mid, even = blk < 2, (blk == 1) | (blk == 2), (blk & 1) == 0
    pay_copies = []
    bounds = [0, 3, 6, packs + 1]
    for part, (begin, end) in enumerate(zip(bounds[:-1], bounds[1:])):
        for j in range(begin, end):
            if j < packs:
                x, w, y, v = (summed(4 * j + c) for c in range(4))
                one = jnp.where(low, x, y) + pltpu.roll(jnp.where(low, y, x), 64, 1)
                two = jnp.where(mid, w, v) + pltpu.roll(jnp.where(mid, v, w), 64, 1)
                put(j, jnp.where(even, one, two) + pltpu.roll(jnp.where(even, two, one), 96, 1))
            else:
                aim = summed(rank)
                aim = aim + pltpu.roll(aim, 64, 1)
                put(j, aim + pltpu.roll(aim, 32, 1))
        for d in range(1, n_item):
            to = lax.rem(me_i + d, n_item)
            copy = pltpu.make_async_remote_copy(
                src_ref=pay.at[to, begin:end], dst_ref=recv.at[d, begin:end],
                send_sem=pay_send.at[part, d], recv_sem=pay_recv.at[part, d],
                device_id={"item": to}, device_id_type=MESH,
            )
            copy.start()
            pay_copies.append(copy)
    for copy in pay_copies:
        copy.wait()
    total = pay[me_i]
    for d in range(1, n_item):
        total = total + recv[d]
    answer = solve([total[j] for j in range(packs)], total[packs])

    xg[me_i] = answer
    x_copies = []
    for d in range(1, n_item):
        copy = pltpu.make_async_remote_copy(
            src_ref=xg.at[me_i], dst_ref=xg.at[me_i], send_sem=x_send.at[d], recv_sem=x_recv.at[d],
            device_id={"item": lax.rem(me_i + d, n_item)}, device_id_type=MESH,
        )
        copy.start()
        x_copies.append(copy)
    for d in range(1, n_item):
        x_copies[d - 1].wait_send()
        source = lax.rem(me_i + n_item - d, n_item)
        pltpu.make_async_remote_copy(
            src_ref=xg.at[source], dst_ref=xg.at[source], send_sem=x_send.at[d], recv_sem=x_recv.at[d],
            device_id={"item": lax.rem(me_i + d, n_item)}, device_id_type=MESH,
        ).wait_recv()
    for q in range(n_item):
        out[q * per : (q + 1) * per, :] = xg[q, 0:per, 0:rank]


def solution(mesh):
    n_user, n_item = mesh.shape["user"], mesh.shape["item"]
    placed = (
        P("user", "item", None, None),
        P("user", "item", None),
        P("user", "item", None),
        P("user", "item", None),
        P("user", "item"),
        P(),
        P(("item", "user"), None),
        P(),
    )

    def local(values, block_user, block_item, block_ctx, block_count, core, item_factor, ctx_factor):
        rank = core.shape[0]
        slots, bw = values.shape[2], values.shape[3]
        packs = rank // 4
        return pl.pallas_call(
            functools.partial(kernel, n_user, n_item),
            out_shape=jax.ShapeDtypeStruct((U_SH, rank), F32),
            in_specs=[pl.BlockSpec(memory_space=pltpu.HBM)] * 8,
            out_specs=pl.BlockSpec(memory_space=pltpu.VMEM),
            scratch_shapes=[
                pltpu.VMEM((slots, bw), BF16),
                pltpu.VMEM((1, slots), jnp.int32),
                pltpu.VMEM((1, slots), jnp.int32),
                pltpu.VMEM((1, slots), jnp.int32),
                pltpu.VMEM((1, 1), jnp.int32),
                pltpu.VMEM(core.shape, BF16),
                pltpu.VMEM((rank, ctx_factor.shape[0]), BF16),
                pltpu.VMEM((n_user, rank, item_factor.shape[0]), BF16),
                pltpu.VMEM((slots, 128), jnp.int32),
                pltpu.VMEM((4, 128, ctx_factor.shape[0]), BF16),
                pltpu.VMEM((packs, slots, 128), BF16),
                pltpu.VMEM(((rank + 2) * slots, bw), F32),
                pltpu.VMEM(((rank + 1) * slots, 128), F32),
                pltpu.VMEM((n_item, packs + 1, 8, 128), F32),
                pltpu.VMEM((n_item, packs + 1, 8, 128), F32),
                pltpu.VMEM((n_item, 8, 128), F32),
                pltpu.SemaphoreType.DMA((8,)),
                pltpu.SemaphoreType.DMA((n_user,)),
                pltpu.SemaphoreType.DMA((n_user,)),
                pltpu.SemaphoreType.DMA((3, n_item)),
                pltpu.SemaphoreType.DMA((3, n_item)),
                pltpu.SemaphoreType.DMA((n_item,)),
                pltpu.SemaphoreType.DMA((n_item,)),
            ],
            compiler_params=pltpu.CompilerParams(
                collective_id=0, has_side_effects=True, vmem_limit_bytes=60 * 1024 * 1024
            ),
        )(
            values, block_user, block_item, block_ctx, block_count, core,
            jnp.transpose(item_factor), jnp.transpose(ctx_factor),
        )

    return jax.shard_map(local, mesh=mesh, in_specs=placed, out_specs=P("user", None), check_vma=False)
```

```python
import functools

import jax
import jax.numpy as jnp
from jax import lax
from jax.experimental import pallas as pl
from jax.experimental.pallas import tpu as pltpu
from jax.sharding import PartitionSpec as P

U_SH = 64
RIDGE = 0.1
MESH = pl.DeviceIdType.MESH
F32 = jnp.float32
BF16 = jnp.bfloat16
NT = (((1,), (1,)), ((), ()))


def iota(shape, dim):
    return lax.broadcasted_iota(jnp.int32, shape, dim)


def lanes_of(x, index):
    return jnp.take_along_axis(x, index, axis=1, mode="promise_in_bounds")


def solve(mats, target):
    shape = mats[0].shape
    lane = iota(shape, 1)
    block, place = lane >> 5, lane & 31
    count = len(mats)
    mats = [m + jnp.where(place == 4 * j + block, RIDGE, 0.0) for j, m in enumerate(mats)]
    cols = [lanes_of(target, 4 * j + block) for j in range(count)]
    own = [jnp.zeros(shape, F32)] * count
    off = [jnp.zeros(shape, F32)] * count
    for k in range(0, 4 * count, 2):
        jk, ck = divmod(k, 4)
        pair = mats[jk]
        p, s, q = (lanes_of(pair, jnp.full(shape, i, jnp.int32)) for i in (ck * 32 + k, ck * 32 + k + 1, ck * 32 + 33 + k))
        row0, row1 = (lanes_of(pair, (ck + i) * 32 + place) for i in (0, 1))
        rhs0, rhs1 = (lanes_of(cols[jk], (ck + i) * 32 + place) for i in (0, 1))
        factor0 = [lanes_of(m, (block << 5) + k) for m in mats]
        factor1 = [lanes_of(m, (block << 5) + k + 1) for m in mats]
        here = (block >> 1) == ck // 2
        factor0[jk], factor1[jk] = jnp.where(here, 0.0, factor0[jk]), jnp.where(here, 0.0, factor1[jk])
        inverse = 1.0 / (p * q - s * s)
        p, s, q = p * inverse, s * inverse, q * inverse
        own[jk] = jnp.where(here, jnp.where((block & 1) == 0, q, p), own[jk])
        off[jk] = jnp.where(here, s, off[jk])
        row0, row1 = q * row0 - s * row1, p * row1 - s * row0
        rhs0, rhs1 = q * rhs0 - s * rhs1, p * rhs1 - s * rhs0
        mats = [m - (f0 * row0 + f1 * row1) for m, f0, f1 in zip(mats, factor0, factor1)]
        cols = [c - (f0 * rhs0 + f1 * rhs1) for c, f0, f1 in zip(cols, factor0, factor1)]
    answer = jnp.zeros(shape, F32)
    for j in range(count):
        x = own[j] * cols[j] - off[j] * lanes_of(cols[j], (block ^ 1) << 5)
        answer = jnp.where((lane >> 2) == j, lanes_of(x, (lane & 3) << 5), answer)
    return answer


def kernel(
    n_user, n_item,
    values_hbm, user_hbm, item_hbm, ctx_hbm, count_hbm, core_hbm, rows_hbm, slab_hbm, out,
    values, b_user, b_item, b_ctx, b_count, core, slab,
    fac, starts, bt, yb, rf, gb, pay, recv, xg,
    load, fac_send, fac_recv, pay_send, pay_recv, x_send, x_recv,
):
    me_u, me_i = lax.axis_index("user"), lax.axis_index("item")
    slots, bw = values.shape
    rank = core.shape[0]
    rows = rows_hbm.shape[1]
    packs = rank // 4
    per = U_SH // n_item
    pitch = slots + 8

    barrier = pltpu.get_barrier_semaphore()
    for d in range(1, n_user):
        pl.semaphore_signal(barrier, inc=1, device_id={"user": lax.rem(me_u + d, n_user)}, device_id_type=MESH)
    for d in range(1, n_item):
        pl.semaphore_signal(barrier, inc=1, device_id={"item": lax.rem(me_i + d, n_item)}, device_id_type=MESH)

    loads = [
        pltpu.make_async_copy(source, target, load.at[i])
        for i, (source, target) in enumerate((
            (ctx_hbm.at[0], b_ctx), (item_hbm.at[0], b_item), (user_hbm.at[0], b_user), (count_hbm, b_count),
            (values_hbm.at[0, 0], values), (rows_hbm, fac.at[0]), (core_hbm, core), (slab_hbm, slab),
        ))
    ]
    for copy in loads:
        copy.start()
    pl.semaphore_wait(barrier, n_user + n_item - 2)
    fac_copies = []
    for d in range(1, n_user):
        copy = pltpu.make_async_remote_copy(
            src_ref=rows_hbm, dst_ref=fac.at[d], send_sem=fac_send.at[d], recv_sem=fac_recv.at[d],
            device_id={"user": lax.rem(me_u + d, n_user)}, device_id_type=MESH,
        )
        copy.start()
        fac_copies.append(copy)
    for copy in loads:
        copy.wait()

    ids = b_item[...]
    parts = [jnp.broadcast_to(r.astype(F32), (128, slots)) for r in (b_ctx[...], ids >> 7, ids & 127)]
    eye = (iota((slots, slots), 0) == iota((slots, slots), 1)).astype(F32).astype(BF16)
    columns = lax.dot_general(eye, jnp.concatenate(parts, axis=0).astype(BF16), NT, preferred_element_type=F32)
    start_col = columns[:, :128].astype(jnp.int32)
    item_col = (columns[:, 128:256] * 128.0 + columns[:, 256:384]).astype(jnp.int32)
    starts[...] = start_col

    turned = values[...].astype(F32)
    for bit in range(bw.bit_length() - 1):
        turned = jnp.where(((start_col >> bit) & 1) == 1, pltpu.roll(turned, 1 << bit, 1), turned)
    rf[pl.ds(rank * pitch, slots), :] = turned
    rf[pl.ds((rank + 1) * pitch, slots), :] = jnp.zeros((slots, bw), F32)

    cores = core[...].astype(F32)
    mixing = jnp.concatenate([cores[a] for a in range(rank)], axis=1).astype(BF16)
    for c in range(4):
        pieces = [jnp.zeros(slab.shape, BF16)] * 4
        pieces[c] = slab[...]
        bt[c] = jnp.concatenate(pieces, axis=0)
    live = iota((U_SH, slots), 1) < b_count[...]
    onehot = jnp.where((iota((U_SH, slots), 0) == b_user[...]) & live, 1.0, 0.0).astype(BF16)

    wanted = jnp.concatenate([item_col] * (rows // 128), axis=1)
    lane = iota((slots, rows), 1)
    chosen = jnp.zeros((slots, rank), F32)
    for d in range(n_user):
        held = lax.rem(me_u + n_user - d, n_user) * rows
        picks = jnp.where(lane + held == wanted, 1.0, 0.0).astype(BF16)
        if d:
            fac_copies[d - 1].wait()
        chosen = chosen + lax.dot_general(picks, fac[d], NT, preferred_element_type=F32)
    proj = jnp.dot(chosen.astype(BF16), mixing, preferred_element_type=F32).astype(BF16)
    for j in range(packs):
        yb[j] = proj[:, 128 * j : 128 * (j + 1)]

    def features(turn, carry):
        first = iota((slots, bw), 1) >= starts[...]
        for i in range(8):
            j, c = 2 * turn + i // 4, i % 4
            full = jnp.dot(yb[j], bt[c], preferred_element_type=F32)
            rf[pl.ds(pl.multiple_of((4 * j + c) * pitch, 8), slots), :] = jnp.where(first, full[:, :bw], full[:, bw:])
        return carry

    lax.fori_loop(0, packs // 2, features, 0)

    unrolled = 8

    def grams(turn, carry):
        sub, ln = iota((8, 128), 0), iota((8, 128), 1)
        low, same = sub < 4, (ln >> 5) == (sub & 3)
        bases = [pl.multiple_of(8 * (unrolled * turn + i), 8) for i in range(unrolled)]
        kept = []
        for base in bases:
            left = jnp.concatenate([rf[pl.ds(a * pitch + base, 8), :] for a in range(rank + 2)], axis=0).astype(BF16)
            right = jnp.concatenate([rf[pl.ds(base + s, rank, stride=pitch), :] for s in range(8)], axis=0).astype(BF16)
            kept.append(lax.dot_general(left, right, NT, preferred_element_type=F32))
        for base, full in zip(bases, kept):
            for a in range(rank + 1):
                part = full[8 * a : 8 * a + 8]
                gb[pl.ds(a * slots + base, 8), :] = jnp.where(same, jnp.where(low, part[:, :128], part[:, 128:]), 0.0)
        return carry

    lax.fori_loop(0, slots // (8 * unrolled), grams, 0)

    def summed(a):
        x = gb[pl.ds(a * slots, slots), :]
        high = x.astype(BF16)
        rest = (x - high.astype(F32)).astype(BF16)
        both = jnp.dot(onehot, jnp.concatenate([high, rest], axis=1), preferred_element_type=F32)
        return both[:, :128] + both[:, 128:]

    if per < 8:
        pay[...] = jnp.zeros(pay.shape, F32)

    def put(j, x):
        for q in range(n_item):
            pay[q, j, 0:per, :] = x[q * per : (q + 1) * per]

    blk = iota((U_SH, 128), 1) >> 5
    low, mid, even = blk < 2, (blk == 1) | (blk == 2), (blk & 1) == 0
    pay_copies = []
    bounds = [0, 4, 7, packs + 1]
    for part, (begin, end) in enumerate(zip(bounds[:-1], bounds[1:])):
        for j in range(begin, end):
            if j:
                x, w, y, v = (summed(4 * j - 4 + c) for c in range(4))
                one = jnp.where(low, x, y) + pltpu.roll(jnp.where(low, y, x), 64, 1)
                two = jnp.where(mid, w, v) + pltpu.roll(jnp.where(mid, v, w), 64, 1)
                put(j, jnp.where(even, one, two) + pltpu.roll(jnp.where(even, two, one), 96, 1))
            else:
                aim = summed(rank)
                aim = aim + pltpu.roll(aim, 64, 1)
                put(j, aim + pltpu.roll(aim, 32, 1))
        for d in range(1, n_item):
            to = lax.rem(me_i + d, n_item)
            copy = pltpu.make_async_remote_copy(
                src_ref=pay.at[to, begin:end], dst_ref=recv.at[d, begin:end],
                send_sem=pay_send.at[part, d], recv_sem=pay_recv.at[part, d],
                device_id={"item": to}, device_id_type=MESH,
            )
            copy.start()
            pay_copies.append(copy)
    for copy in pay_copies:
        copy.wait()
    total = pay[me_i]
    for d in range(1, n_item):
        total = total + recv[d]
    answer = solve([total[j + 1] for j in range(packs)], total[0])

    xg[me_i] = answer
    x_copies = []
    for d in range(1, n_item):
        copy = pltpu.make_async_remote_copy(
            src_ref=xg.at[me_i], dst_ref=xg.at[me_i], send_sem=x_send.at[d], recv_sem=x_recv.at[d],
            device_id={"item": lax.rem(me_i + d, n_item)}, device_id_type=MESH,
        )
        copy.start()
        x_copies.append(copy)
    for d in range(1, n_item):
        x_copies[d - 1].wait_send()
        source = lax.rem(me_i + n_item - d, n_item)
        pltpu.make_async_remote_copy(
            src_ref=xg.at[source], dst_ref=xg.at[source], send_sem=x_send.at[d], recv_sem=x_recv.at[d],
            device_id={"item": lax.rem(me_i + d, n_item)}, device_id_type=MESH,
        ).wait_recv()
    solved = jnp.concatenate([xg[q, 0:per, :] for q in range(n_item)] + [jnp.zeros((128 - U_SH, 128), F32)], axis=0)
    out[...] = jnp.transpose(solved)[:rank, :U_SH]


def solution(mesh):
    n_user, n_item = mesh.shape["user"], mesh.shape["item"]
    placed = (
        P("user", "item", None, None),
        P("user", "item", None),
        P("user", "item", None),
        P("user", "item", None),
        P("user", "item"),
        P(),
        P(("item", "user"), None),
        P(),
    )

    def local(values, block_user, block_item, block_ctx, block_count, core, item_factor, ctx_factor):
        rank = core.shape[0]
        slots, bw = values.shape[2], values.shape[3]
        packs = rank // 4
        solved = pl.pallas_call(
            functools.partial(kernel, n_user, n_item),
            out_shape=jax.ShapeDtypeStruct((rank, U_SH), F32),
            in_specs=[pl.BlockSpec(memory_space=pltpu.HBM)] * 8,
            out_specs=pl.BlockSpec(memory_space=pltpu.VMEM),
            scratch_shapes=[
                pltpu.VMEM((slots, bw), BF16),
                pltpu.VMEM((1, slots), jnp.int32),
                pltpu.VMEM((1, slots), jnp.int32),
                pltpu.VMEM((1, slots), jnp.int32),
                pltpu.VMEM((1, 1), jnp.int32),
                pltpu.VMEM(core.shape, BF16),
                pltpu.VMEM((rank, ctx_factor.shape[0]), BF16),
                pltpu.VMEM((n_user, rank, item_factor.shape[0]), BF16),
                pltpu.VMEM((slots, 128), jnp.int32),
                pltpu.VMEM((4, 128, ctx_factor.shape[0]), BF16),
                pltpu.VMEM((packs, slots, 128), BF16),
                pltpu.VMEM(((rank + 2) * (slots + 8), bw), F32),
                pltpu.VMEM(((rank + 1) * slots, 128), F32),
                pltpu.VMEM((n_item, packs + 1, 8, 128), F32),
                pltpu.VMEM((n_item, packs + 1, 8, 128), F32),
                pltpu.VMEM((n_item, 8, 128), F32),
                pltpu.SemaphoreType.DMA((8,)),
                pltpu.SemaphoreType.DMA((n_user,)),
                pltpu.SemaphoreType.DMA((n_user,)),
                pltpu.SemaphoreType.DMA((3, n_item)),
                pltpu.SemaphoreType.DMA((3, n_item)),
                pltpu.SemaphoreType.DMA((n_item,)),
                pltpu.SemaphoreType.DMA((n_item,)),
            ],
            compiler_params=pltpu.CompilerParams(
                collective_id=0, has_side_effects=True, vmem_limit_bytes=60 * 1024 * 1024
            ),
        )(
            values, block_user, block_item, block_ctx, block_count, core,
            jnp.transpose(item_factor), jnp.transpose(ctx_factor),
        )
        return jnp.transpose(solved)

    return jax.shard_map(local, mesh=mesh, in_specs=placed, out_specs=P("user", None), check_vma=False)
```

```python
import functools

import jax
import jax.numpy as jnp
from jax import lax
from jax.experimental import pallas as pl
from jax.experimental.pallas import tpu as pltpu
from jax.sharding import PartitionSpec as P

U_SH = 64
RIDGE = 0.1
MESH = pl.DeviceIdType.MESH
F32 = jnp.float32
BF16 = jnp.bfloat16
NT = (((1,), (1,)), ((), ()))


def iota(shape, dim):
    return lax.broadcasted_iota(jnp.int32, shape, dim)


def lanes_of(x, index):
    return jnp.take_along_axis(x, index, axis=1, mode="promise_in_bounds")


def solve(mats, target):
    shape = mats[0].shape
    lane = iota(shape, 1)
    block, place = lane >> 5, lane & 31
    count = len(mats)
    mats = [m + jnp.where(place == 4 * j + block, RIDGE, 0.0) for j, m in enumerate(mats)]
    cols = [lanes_of(target, 4 * j + block) for j in range(count)]
    own = [jnp.zeros(shape, F32)] * count
    off = [jnp.zeros(shape, F32)] * count
    for k in range(0, 4 * count, 2):
        jk, ck = divmod(k, 4)
        pair = mats[jk]
        p, s, q = (lanes_of(pair, jnp.full(shape, i, jnp.int32)) for i in (ck * 32 + k, ck * 32 + k + 1, ck * 32 + 33 + k))
        row0, row1 = (lanes_of(pair, (ck + i) * 32 + place) for i in (0, 1))
        rhs0, rhs1 = (lanes_of(cols[jk], (ck + i) * 32 + place) for i in (0, 1))
        factor0 = [lanes_of(m, (block << 5) + k) for m in mats]
        factor1 = [lanes_of(m, (block << 5) + k + 1) for m in mats]
        here = (block >> 1) == ck // 2
        factor0[jk], factor1[jk] = jnp.where(here, 0.0, factor0[jk]), jnp.where(here, 0.0, factor1[jk])
        inverse = 1.0 / (p * q - s * s)
        p, s, q = p * inverse, s * inverse, q * inverse
        own[jk] = jnp.where(here, jnp.where((block & 1) == 0, q, p), own[jk])
        off[jk] = jnp.where(here, s, off[jk])
        row0, row1 = q * row0 - s * row1, p * row1 - s * row0
        rhs0, rhs1 = q * rhs0 - s * rhs1, p * rhs1 - s * rhs0
        mats = [m - (f0 * row0 + f1 * row1) for m, f0, f1 in zip(mats, factor0, factor1)]
        cols = [c - (f0 * rhs0 + f1 * rhs1) for c, f0, f1 in zip(cols, factor0, factor1)]
    answer = jnp.zeros(shape, F32)
    for j in range(count):
        x = own[j] * cols[j] - off[j] * lanes_of(cols[j], (block ^ 1) << 5)
        answer = jnp.where((lane >> 2) == j, lanes_of(x, (lane & 3) << 5), answer)
    return answer


def kernel(
    n_user, n_item,
    values_hbm, user_hbm, item_hbm, ctx_hbm, count_hbm, core_hbm, rows_hbm, slab_hbm, out,
    values, b_user, b_item, b_ctx, b_count, core, slab,
    fac, starts, bt, yb, rf, gb, pay, recv, xg,
    load, fac_send, fac_recv, pay_send, pay_recv, x_send, x_recv,
):
    me_u, me_i = lax.axis_index("user"), lax.axis_index("item")
    slots, bw = values.shape
    rank = core.shape[0]
    rows = rows_hbm.shape[1]
    packs = rank // 4
    per = U_SH // n_item
    pitch = slots + 8

    barrier = pltpu.get_barrier_semaphore()
    for d in range(1, n_user):
        pl.semaphore_signal(barrier, inc=1, device_id={"user": lax.rem(me_u + d, n_user)}, device_id_type=MESH)
    for d in range(1, n_item):
        pl.semaphore_signal(barrier, inc=1, device_id={"item": lax.rem(me_i + d, n_item)}, device_id_type=MESH)

    loads = [
        pltpu.make_async_copy(source, target, load.at[i])
        for i, (source, target) in enumerate((
            (ctx_hbm.at[0], b_ctx), (item_hbm.at[0], b_item), (user_hbm.at[0], b_user), (count_hbm, b_count),
            (values_hbm.at[0, 0], values), (rows_hbm, fac.at[0]), (core_hbm, core), (slab_hbm, slab),
        ))
    ]
    for copy in loads:
        copy.start()
    pl.semaphore_wait(barrier, n_user + n_item - 2)
    fac_copies = []
    for d in range(1, n_user):
        copy = pltpu.make_async_remote_copy(
            src_ref=rows_hbm, dst_ref=fac.at[d], send_sem=fac_send.at[d], recv_sem=fac_recv.at[d],
            device_id={"user": lax.rem(me_u + d, n_user)}, device_id_type=MESH,
        )
        copy.start()
        fac_copies.append(copy)
    for copy in loads:
        copy.wait()

    ids = b_item[...]
    parts = [jnp.broadcast_to(r.astype(F32), (128, slots)) for r in (b_ctx[...], ids >> 7, ids & 127)]
    eye = (iota((slots, slots), 0) == iota((slots, slots), 1)).astype(F32).astype(BF16)
    columns = lax.dot_general(eye, jnp.concatenate(parts, axis=0).astype(BF16), NT, preferred_element_type=F32)
    start_col = columns[:, :128].astype(jnp.int32)
    item_col = (columns[:, 128:256] * 128.0 + columns[:, 256:384]).astype(jnp.int32)
    starts[...] = start_col

    turned = values[...].astype(F32)
    for bit in range(bw.bit_length() - 1):
        turned = jnp.where(((start_col >> bit) & 1) == 1, pltpu.roll(turned, 1 << bit, 1), turned)
    rf[pl.ds(rank * pitch, slots), :] = turned
    rf[pl.ds((rank + 1) * pitch, slots), :] = jnp.zeros((slots, bw), F32)

    cores = core[...].astype(F32)
    mixing = jnp.concatenate([cores[a] for a in range(rank)], axis=1).astype(BF16)
    for c in range(4):
        pieces = [jnp.zeros(slab.shape, BF16)] * 4
        pieces[c] = slab[...]
        bt[c] = jnp.concatenate(pieces, axis=0)
    live = iota((U_SH, slots), 1) < b_count[...]
    onehot = jnp.where((iota((U_SH, slots), 0) == b_user[...]) & live, 1.0, 0.0).astype(BF16)

    wanted = jnp.concatenate([item_col] * (rows // 128), axis=1)
    lane = iota((slots, rows), 1)
    chosen = jnp.zeros((slots, rank), F32)
    for d in range(n_user):
        held = lax.rem(me_u + n_user - d, n_user) * rows
        picks = jnp.where(lane + held == wanted, 1.0, 0.0).astype(BF16)
        if d:
            fac_copies[d - 1].wait()
        chosen = chosen + lax.dot_general(picks, fac[d], NT, preferred_element_type=F32)
    proj = jnp.dot(chosen.astype(BF16), mixing, preferred_element_type=F32).astype(BF16)
    for j in range(packs):
        yb[j] = proj[:, 128 * j : 128 * (j + 1)]

    def features(turn, carry):
        first = iota((slots, bw), 1) >= starts[...]
        for i in range(8):
            j, c = 2 * turn + i // 4, i % 4
            full = jnp.dot(yb[j], bt[c], preferred_element_type=F32)
            rf[pl.ds(pl.multiple_of((4 * j + c) * pitch, 8), slots), :] = jnp.where(first, full[:, :bw], full[:, bw:])
        return carry

    lax.fori_loop(0, packs // 2, features, 0)

    turns = 2

    def grams(turn, carry):
        sub, ln = iota((8, 128), 0), iota((8, 128), 1)
        low, same = sub < 4, (ln >> 5) == (sub & 3)
        for i in range(turns):
            base = pl.multiple_of(16 * (turns * turn + i), 16)
            kept = []
            for begin in (base, base + 8):
                left = jnp.concatenate([rf[pl.ds(a * pitch + begin, 8), :] for a in range(rank + 2)], axis=0).astype(BF16)
                right = jnp.concatenate([rf[pl.ds(begin + s, rank, stride=pitch), :] for s in range(8)], axis=0).astype(BF16)
                kept.append(lax.dot_general(left, right, NT, preferred_element_type=F32))
            for a in range(rank + 1):
                parts = [full[8 * a : 8 * a + 8] for full in kept]
                parts = [jnp.where(same, jnp.where(low, p[:, :128], p[:, 128:]), 0.0) for p in parts]
                part = jnp.concatenate(parts, axis=0)
                high = part.astype(BF16)
                gb[a, pl.ds(base, 16), 0:128] = high
                gb[a, pl.ds(base, 16), 128:256] = (part - high.astype(F32)).astype(BF16)
        return carry

    lax.fori_loop(0, slots // (16 * turns), grams, 0)

    def summed(a):
        both = jnp.dot(onehot, gb[a], preferred_element_type=F32)
        return both[:, :128] + both[:, 128:]

    if per < 8:
        pay[...] = jnp.zeros(pay.shape, F32)

    def put(j, x):
        for q in range(n_item):
            pay[q, j, 0:per, :] = x[q * per : (q + 1) * per]

    blk = iota((U_SH, 128), 1) >> 5
    low, mid, even = blk < 2, (blk == 1) | (blk == 2), (blk & 1) == 0
    pay_copies = []
    bounds = [0, 4, 7, packs + 1]
    for part, (begin, end) in enumerate(zip(bounds[:-1], bounds[1:])):
        for j in range(begin, end):
            if j:
                x, w, y, v = (summed(4 * j - 4 + c) for c in range(4))
                one = jnp.where(low, x, y) + pltpu.roll(jnp.where(low, y, x), 64, 1)
                two = jnp.where(mid, w, v) + pltpu.roll(jnp.where(mid, v, w), 64, 1)
                put(j, jnp.where(even, one, two) + pltpu.roll(jnp.where(even, two, one), 96, 1))
            else:
                aim = summed(rank)
                aim = aim + pltpu.roll(aim, 64, 1)
                put(j, aim + pltpu.roll(aim, 32, 1))
        for d in range(1, n_item):
            to = lax.rem(me_i + d, n_item)
            copy = pltpu.make_async_remote_copy(
                src_ref=pay.at[to, begin:end], dst_ref=recv.at[d, begin:end],
                send_sem=pay_send.at[part, d], recv_sem=pay_recv.at[part, d],
                device_id={"item": to}, device_id_type=MESH,
            )
            copy.start()
            pay_copies.append(copy)
    for copy in pay_copies:
        copy.wait()
    total = pay[me_i]
    for d in range(1, n_item):
        total = total + recv[d]
    answer = solve([total[j + 1] for j in range(packs)], total[0])

    xg[me_i] = answer
    x_copies = []
    for d in range(1, n_item):
        copy = pltpu.make_async_remote_copy(
            src_ref=xg.at[me_i], dst_ref=xg.at[me_i], send_sem=x_send.at[d], recv_sem=x_recv.at[d],
            device_id={"item": lax.rem(me_i + d, n_item)}, device_id_type=MESH,
        )
        copy.start()
        x_copies.append(copy)
    for d in range(1, n_item):
        x_copies[d - 1].wait_send()
        source = lax.rem(me_i + n_item - d, n_item)
        pltpu.make_async_remote_copy(
            src_ref=xg.at[source], dst_ref=xg.at[source], send_sem=x_send.at[d], recv_sem=x_recv.at[d],
            device_id={"item": lax.rem(me_i + d, n_item)}, device_id_type=MESH,
        ).wait_recv()
    solved = jnp.concatenate([xg[q, 0:per, :] for q in range(n_item)] + [jnp.zeros((128 - U_SH, 128), F32)], axis=0)
    out[...] = jnp.transpose(solved)[:rank, :U_SH]


def solution(mesh):
    n_user, n_item = mesh.shape["user"], mesh.shape["item"]
    placed = (
        P("user", "item", None, None),
        P("user", "item", None),
        P("user", "item", None),
        P("user", "item", None),
        P("user", "item"),
        P(),
        P(("item", "user"), None),
        P(),
    )

    def local(values, block_user, block_item, block_ctx, block_count, core, item_factor, ctx_factor):
        rank = core.shape[0]
        slots, bw = values.shape[2], values.shape[3]
        packs = rank // 4
        solved = pl.pallas_call(
            functools.partial(kernel, n_user, n_item),
            out_shape=jax.ShapeDtypeStruct((rank, U_SH), F32),
            in_specs=[pl.BlockSpec(memory_space=pltpu.HBM)] * 8,
            out_specs=pl.BlockSpec(memory_space=pltpu.VMEM),
            scratch_shapes=[
                pltpu.VMEM((slots, bw), BF16),
                pltpu.VMEM((1, slots), jnp.int32),
                pltpu.VMEM((1, slots), jnp.int32),
                pltpu.VMEM((1, slots), jnp.int32),
                pltpu.VMEM((1, 1), jnp.int32),
                pltpu.VMEM(core.shape, BF16),
                pltpu.VMEM((rank, ctx_factor.shape[0]), BF16),
                pltpu.VMEM((n_user, rank, item_factor.shape[0]), BF16),
                pltpu.VMEM((slots, 128), jnp.int32),
                pltpu.VMEM((4, 128, ctx_factor.shape[0]), BF16),
                pltpu.VMEM((packs, slots, 128), BF16),
                pltpu.VMEM(((rank + 2) * (slots + 8), bw), F32),
                pltpu.VMEM((rank + 1, slots, 256), BF16),
                pltpu.VMEM((n_item, packs + 1, 8, 128), F32),
                pltpu.VMEM((n_item, packs + 1, 8, 128), F32),
                pltpu.VMEM((n_item, 8, 128), F32),
                pltpu.SemaphoreType.DMA((8,)),
                pltpu.SemaphoreType.DMA((n_user,)),
                pltpu.SemaphoreType.DMA((n_user,)),
                pltpu.SemaphoreType.DMA((3, n_item)),
                pltpu.SemaphoreType.DMA((3, n_item)),
                pltpu.SemaphoreType.DMA((n_item,)),
                pltpu.SemaphoreType.DMA((n_item,)),
            ],
            compiler_params=pltpu.CompilerParams(
                collective_id=0, has_side_effects=True, vmem_limit_bytes=60 * 1024 * 1024
            ),
        )(
            values, block_user, block_item, block_ctx, block_count, core,
            jnp.transpose(item_factor), jnp.transpose(ctx_factor),
        )
        return jnp.transpose(solved)

    return jax.shard_map(local, mesh=mesh, in_specs=placed, out_specs=P("user", None), check_vma=False)
```

```python
import functools

import jax
import jax.numpy as jnp
from jax import lax
from jax.experimental import pallas as pl
from jax.experimental.pallas import tpu as pltpu
from jax.sharding import PartitionSpec as P

U_SH = 64
RIDGE = 0.1
MESH = pl.DeviceIdType.MESH
F32 = jnp.float32
BF16 = jnp.bfloat16
NT = (((1,), (1,)), ((), ()))


def iota(shape, dim):
    return lax.broadcasted_iota(jnp.int32, shape, dim)


def lanes_of(x, index):
    return jnp.take_along_axis(x, index, axis=1, mode="promise_in_bounds")


def in_hbm(x):
    return pltpu.with_memory_space_constraint(x, pltpu.HBM)


def solve(mats, target):
    shape = mats[0].shape
    lane = iota(shape, 1)
    block, place = lane >> 5, lane & 31
    count = len(mats)
    mats = [m + jnp.where(place == 4 * j + block, RIDGE, 0.0) for j, m in enumerate(mats)]
    cols = [lanes_of(target, 4 * j + block) for j in range(count)]
    own = [jnp.zeros(shape, F32)] * count
    off = [jnp.zeros(shape, F32)] * count
    for k in range(0, 4 * count, 2):
        jk, ck = divmod(k, 4)
        pair = mats[jk]
        p, s, q = (lanes_of(pair, jnp.full(shape, i, jnp.int32)) for i in (ck * 32 + k, ck * 32 + k + 1, ck * 32 + 33 + k))
        row0, row1 = (lanes_of(pair, (ck + i) * 32 + place) for i in (0, 1))
        rhs0, rhs1 = (lanes_of(cols[jk], (ck + i) * 32 + place) for i in (0, 1))
        factor0 = [lanes_of(m, (block << 5) + k) for m in mats]
        factor1 = [lanes_of(m, (block << 5) + k + 1) for m in mats]
        here = (block >> 1) == ck // 2
        factor0[jk], factor1[jk] = jnp.where(here, 0.0, factor0[jk]), jnp.where(here, 0.0, factor1[jk])
        inverse = 1.0 / (p * q - s * s)
        p, s, q = p * inverse, s * inverse, q * inverse
        own[jk] = jnp.where(here, jnp.where((block & 1) == 0, q, p), own[jk])
        off[jk] = jnp.where(here, s, off[jk])
        row0, row1 = q * row0 - s * row1, p * row1 - s * row0
        rhs0, rhs1 = q * rhs0 - s * rhs1, p * rhs1 - s * rhs0
        mats = [m - (f0 * row0 + f1 * row1) for m, f0, f1 in zip(mats, factor0, factor1)]
        cols = [c - (f0 * rhs0 + f1 * rhs1) for c, f0, f1 in zip(cols, factor0, factor1)]
    answer = jnp.zeros(shape, F32)
    for j in range(count):
        x = own[j] * cols[j] - off[j] * lanes_of(cols[j], (block ^ 1) << 5)
        answer = jnp.where((lane >> 2) == j, lanes_of(x, (lane & 3) << 5), answer)
    return answer


def kernel(
    n_user, n_item,
    values_hbm, user_hbm, item_hbm, ctx_hbm, count_hbm, core_hbm, rows_hbm, slab_hbm, out,
    values, b_user, b_item, b_ctx, b_count, core, slab,
    fac, starts, bt, yb, rf, gb, pay, recv, xg,
    load, fac_send, fac_recv, pay_send, pay_recv, x_send, x_recv,
):
    me_u, me_i = lax.axis_index("user"), lax.axis_index("item")
    slots, bw = values.shape
    rank = core.shape[0]
    rows = rows_hbm.shape[1]
    packs = rank // 4
    per = U_SH // n_item
    pitch = slots + 8

    barrier = pltpu.get_barrier_semaphore()
    for d in range(1, n_user):
        pl.semaphore_signal(barrier, inc=1, device_id={"user": lax.rem(me_u + d, n_user)}, device_id_type=MESH)
    for d in range(1, n_item):
        pl.semaphore_signal(barrier, inc=1, device_id={"item": lax.rem(me_i + d, n_item)}, device_id_type=MESH)

    loads = [
        pltpu.make_async_copy(source, target, load.at[i])
        for i, (source, target) in enumerate((
            (ctx_hbm.at[0], b_ctx), (item_hbm.at[0], b_item), (user_hbm.at[0], b_user), (count_hbm, b_count),
            (values_hbm.at[0, 0], values), (rows_hbm, fac.at[0]), (core_hbm, core), (slab_hbm, slab),
        ))
    ]
    for copy in loads:
        copy.start()
    pl.semaphore_wait(barrier, n_user + n_item - 2)
    fac_copies = []
    for d in range(1, n_user):
        copy = pltpu.make_async_remote_copy(
            src_ref=rows_hbm, dst_ref=fac.at[d], send_sem=fac_send.at[d], recv_sem=fac_recv.at[d],
            device_id={"user": lax.rem(me_u + d, n_user)}, device_id_type=MESH,
        )
        copy.start()
        fac_copies.append(copy)
    for copy in loads:
        copy.wait()

    ids = b_item[...]
    parts = [jnp.broadcast_to(r.astype(F32), (128, slots)) for r in (b_ctx[...], ids >> 7, ids & 127)]
    eye = (iota((slots, slots), 0) == iota((slots, slots), 1)).astype(F32).astype(BF16)
    columns = lax.dot_general(eye, jnp.concatenate(parts, axis=0).astype(BF16), NT, preferred_element_type=F32)
    start_col = columns[:, :128].astype(jnp.int32)
    item_col = (columns[:, 128:256] * 128.0 + columns[:, 256:384]).astype(jnp.int32)
    starts[...] = start_col

    turned = values[...].astype(F32)
    for bit in range(bw.bit_length() - 1):
        turned = jnp.where(((start_col >> bit) & 1) == 1, pltpu.roll(turned, 1 << bit, 1), turned)
    rf[pl.ds(rank * pitch, slots), :] = turned
    rf[pl.ds((rank + 1) * pitch, slots), :] = jnp.zeros((slots, bw), F32)

    cores = core[...].astype(F32)
    mixing = jnp.concatenate([cores[a] for a in range(rank)], axis=1).astype(BF16)
    for c in range(4):
        pieces = [jnp.zeros(slab.shape, BF16)] * 4
        pieces[c] = slab[...]
        bt[c] = jnp.concatenate(pieces, axis=0)
    live = iota((U_SH, slots), 1) < b_count[...]
    onehot = jnp.where((iota((U_SH, slots), 0) == b_user[...]) & live, 1.0, 0.0).astype(BF16)

    wanted = jnp.concatenate([item_col] * (rows // 128), axis=1)
    lane = iota((slots, rows), 1)
    chosen = jnp.zeros((slots, rank), F32)
    for d in range(n_user):
        held = lax.rem(me_u + n_user - d, n_user) * rows
        picks = jnp.where(lane + held == wanted, 1.0, 0.0).astype(BF16)
        if d:
            fac_copies[d - 1].wait()
        chosen = chosen + lax.dot_general(picks, fac[d], NT, preferred_element_type=F32)
    proj = jnp.dot(chosen.astype(BF16), mixing, preferred_element_type=F32).astype(BF16)
    for j in range(packs):
        yb[j] = proj[:, 128 * j : 128 * (j + 1)]

    def features(turn, carry):
        first = iota((slots, bw), 1) >= starts[...]
        for i in range(rank):
            j, c = i // 4, i % 4
            full = jnp.dot(yb[j], bt[c], preferred_element_type=F32)
            rf[pl.ds((4 * j + c) * pitch, slots), :] = jnp.where(first, full[:, :bw], full[:, bw:])
        return carry

    features(0, 0)

    unrolled = slots // 8

    def grams(turn, carry):
        sub, ln = iota((8, 128), 0), iota((8, 128), 1)
        low, same = sub < 4, (ln >> 5) == (sub & 3)
        bases = [8 * i for i in range(unrolled)]
        for base in bases:
            left = jnp.concatenate([rf[pl.ds(a * pitch + base, 8), :] for a in range(rank + 2)], axis=0).astype(BF16)
            right = jnp.concatenate([rf[pl.ds(base + s, rank, stride=pitch), :] for s in range(8)], axis=0).astype(BF16)
            full = lax.dot_general(left, right, NT, preferred_element_type=F32)
            for a in range(rank + 1):
                part = full[8 * a : 8 * a + 8]
                gb[pl.ds(a * slots + base, 8), :] = jnp.where(same, jnp.where(low, part[:, :128], part[:, 128:]), 0.0)
        return carry

    grams(0, 0)

    def summed(a):
        x = gb[pl.ds(a * slots, slots), :]
        high = x.astype(BF16)
        rest = (x - high.astype(F32)).astype(BF16)
        both = jnp.dot(onehot, jnp.concatenate([high, rest], axis=1), preferred_element_type=F32)
        return both[:, :128] + both[:, 128:]

    if per < 8:
        pay[...] = jnp.zeros(pay.shape, F32)

    def put(j, x):
        for q in range(n_item):
            pay[q, j, 0:per, :] = x[q * per : (q + 1) * per]

    blk = iota((U_SH, 128), 1) >> 5
    low, mid, even = blk < 2, (blk == 1) | (blk == 2), (blk & 1) == 0
    pay_copies = []
    bounds = [0, 4, 7, packs + 1]
    for part, (begin, end) in enumerate(zip(bounds[:-1], bounds[1:])):
        for j in range(begin, end):
            if j:
                x, w, y, v = (summed(4 * j - 4 + c) for c in range(4))
                one = jnp.where(low, x, y) + pltpu.roll(jnp.where(low, y, x), 64, 1)
                two = jnp.where(mid, w, v) + pltpu.roll(jnp.where(mid, v, w), 64, 1)
                put(j, jnp.where(even, one, two) + pltpu.roll(jnp.where(even, two, one), 96, 1))
            else:
                aim = summed(rank)
                aim = aim + pltpu.roll(aim, 64, 1)
                put(j, aim + pltpu.roll(aim, 32, 1))
        for d in range(1, n_item):
            to = lax.rem(me_i + d, n_item)
            copy = pltpu.make_async_remote_copy(
                src_ref=pay.at[to, begin:end], dst_ref=recv.at[d, begin:end],
                send_sem=pay_send.at[part, d], recv_sem=pay_recv.at[part, d],
                device_id={"item": to}, device_id_type=MESH,
            )
            copy.start()
            pay_copies.append(copy)
    for copy in pay_copies:
        copy.wait()
    total = pay[me_i]
    for d in range(1, n_item):
        total = total + recv[d]
    answer = solve([total[j + 1] for j in range(packs)], total[0])

    xg[me_i] = answer
    x_copies = []
    for d in range(1, n_item):
        copy = pltpu.make_async_remote_copy(
            src_ref=xg.at[me_i], dst_ref=xg.at[me_i], send_sem=x_send.at[d], recv_sem=x_recv.at[d],
            device_id={"item": lax.rem(me_i + d, n_item)}, device_id_type=MESH,
        )
        copy.start()
        x_copies.append(copy)
    for d in range(1, n_item):
        x_copies[d - 1].wait_send()
        source = lax.rem(me_i + n_item - d, n_item)
        pltpu.make_async_remote_copy(
            src_ref=xg.at[source], dst_ref=xg.at[source], send_sem=x_send.at[d], recv_sem=x_recv.at[d],
            device_id={"item": lax.rem(me_i + d, n_item)}, device_id_type=MESH,
        ).wait_recv()
    solved = jnp.concatenate([xg[q, 0:per, :] for q in range(n_item)] + [jnp.zeros((128 - U_SH, 128), F32)], axis=0)
    out[...] = jnp.transpose(solved)[:rank, :U_SH]


def solution(mesh):
    n_user, n_item = mesh.shape["user"], mesh.shape["item"]
    placed = (
        P("user", "item", None, None),
        P("user", "item", None),
        P("user", "item", None),
        P("user", "item", None),
        P("user", "item"),
        P(),
        P(("item", "user"), None),
        P(),
    )

    def local(values, block_user, block_item, block_ctx, block_count, core, item_factor, ctx_factor):
        rank = core.shape[0]
        slots, bw = values.shape[2], values.shape[3]
        packs = rank // 4
        solved = pl.pallas_call(
            functools.partial(kernel, n_user, n_item),
            out_shape=pltpu.VMEM((rank, U_SH), F32),
            in_specs=[pl.BlockSpec(memory_space=pltpu.HBM)] * 8,
            out_specs=pl.BlockSpec(memory_space=pltpu.VMEM),
            scratch_shapes=[
                pltpu.VMEM((slots, bw), BF16),
                pltpu.VMEM((1, slots), jnp.int32),
                pltpu.VMEM((1, slots), jnp.int32),
                pltpu.VMEM((1, slots), jnp.int32),
                pltpu.VMEM((1, 1), jnp.int32),
                pltpu.VMEM(core.shape, BF16),
                pltpu.VMEM((rank, ctx_factor.shape[0]), BF16),
                pltpu.VMEM((n_user, rank, item_factor.shape[0]), BF16),
                pltpu.VMEM((slots, 128), jnp.int32),
                pltpu.VMEM((4, 128, ctx_factor.shape[0]), BF16),
                pltpu.VMEM((packs, slots, 128), BF16),
                pltpu.VMEM(((rank + 2) * (slots + 8), bw), F32),
                pltpu.VMEM(((rank + 1) * slots, 128), F32),
                pltpu.VMEM((n_item, packs + 1, 8, 128), F32),
                pltpu.VMEM((n_item, packs + 1, 8, 128), F32),
                pltpu.VMEM((n_item, 8, 128), F32),
                pltpu.SemaphoreType.DMA((8,)),
                pltpu.SemaphoreType.DMA((n_user,)),
                pltpu.SemaphoreType.DMA((n_user,)),
                pltpu.SemaphoreType.DMA((3, n_item)),
                pltpu.SemaphoreType.DMA((3, n_item)),
                pltpu.SemaphoreType.DMA((n_item,)),
                pltpu.SemaphoreType.DMA((n_item,)),
            ],
            compiler_params=pltpu.CompilerParams(
                collective_id=0, has_side_effects=True, vmem_limit_bytes=48 * 1024 * 1024
            ),
        )(
            *(in_hbm(x) for x in (values, block_user, block_item, block_ctx)), block_count,
            *(in_hbm(x) for x in (core, jnp.transpose(item_factor), jnp.transpose(ctx_factor))),
        )
        return jnp.transpose(solved)

    return jax.shard_map(local, mesh=mesh, in_specs=placed, out_specs=P("user", None), check_vma=False)
```

```python
import functools

import jax
import jax.numpy as jnp
from jax import lax
from jax.experimental import pallas as pl
from jax.experimental.pallas import tpu as pltpu
from jax.sharding import PartitionSpec as P

U_SH = 64
RIDGE = 0.1
MESH = pl.DeviceIdType.MESH
F32 = jnp.float32
BF16 = jnp.bfloat16
NT = (((1,), (1,)), ((), ()))


def iota(shape, dim):
    return lax.broadcasted_iota(jnp.int32, shape, dim)


def lanes_of(x, index):
    return jnp.take_along_axis(x, index, axis=1, mode="promise_in_bounds")


def in_hbm(x):
    return pltpu.with_memory_space_constraint(x, pltpu.HBM)


def solve(mats, target):
    shape = mats[0].shape
    lane = iota(shape, 1)
    block, place = lane >> 5, lane & 31
    count = len(mats)
    mats = [m + jnp.where(place == 4 * j + block, RIDGE, 0.0) for j, m in enumerate(mats)]
    cols = [lanes_of(target, 4 * j + block) for j in range(count)]
    own = [jnp.zeros(shape, F32)] * count
    off = [jnp.zeros(shape, F32)] * count
    for k in range(0, 4 * count, 2):
        jk, ck = divmod(k, 4)
        pair = mats[jk]
        p, s, q = (lanes_of(pair, jnp.full(shape, i, jnp.int32)) for i in (ck * 32 + k, ck * 32 + k + 1, ck * 32 + 33 + k))
        row0, row1 = (lanes_of(pair, (ck + i) * 32 + place) for i in (0, 1))
        rhs0, rhs1 = (lanes_of(cols[jk], (ck + i) * 32 + place) for i in (0, 1))
        factor0 = [lanes_of(m, (block << 5) + k) for m in mats]
        factor1 = [lanes_of(m, (block << 5) + k + 1) for m in mats]
        here = (block >> 1) == ck // 2
        factor0[jk], factor1[jk] = jnp.where(here, 0.0, factor0[jk]), jnp.where(here, 0.0, factor1[jk])
        inverse = 1.0 / (p * q - s * s)
        p, s, q = p * inverse, s * inverse, q * inverse
        own[jk] = jnp.where(here, jnp.where((block & 1) == 0, q, p), own[jk])
        off[jk] = jnp.where(here, s, off[jk])
        row0, row1 = q * row0 - s * row1, p * row1 - s * row0
        rhs0, rhs1 = q * rhs0 - s * rhs1, p * rhs1 - s * rhs0
        mats = [m - (f0 * row0 + f1 * row1) for m, f0, f1 in zip(mats, factor0, factor1)]
        cols = [c - (f0 * rhs0 + f1 * rhs1) for c, f0, f1 in zip(cols, factor0, factor1)]
    answer = jnp.zeros(shape, F32)
    for j in range(count):
        x = own[j] * cols[j] - off[j] * lanes_of(cols[j], (block ^ 1) << 5)
        answer = jnp.where((lane >> 2) == j, lanes_of(x, (lane & 3) << 5), answer)
    return answer


def kernel(
    n_user, n_item,
    values_hbm, user_hbm, item_hbm, ctx_hbm, count_hbm, core_hbm, rows_hbm, slab_hbm, out,
    values, b_user, b_item, b_ctx, b_count, core, slab,
    fac, starts, bt, yb, rf, gb, pay, recv, xg,
    load, fac_send, fac_recv, pay_send, pay_recv, x_send, x_recv,
):
    me_u, me_i = lax.axis_index("user"), lax.axis_index("item")
    slots, bw = values.shape
    rank = core.shape[0]
    rows = rows_hbm.shape[1]
    packs = rank // 4
    per = U_SH // n_item
    pitch = slots + 8

    barrier = pltpu.get_barrier_semaphore()
    for d in range(1, n_user):
        pl.semaphore_signal(barrier, inc=1, device_id={"user": lax.rem(me_u + d, n_user)}, device_id_type=MESH)
    for d in range(1, n_item):
        pl.semaphore_signal(barrier, inc=1, device_id={"item": lax.rem(me_i + d, n_item)}, device_id_type=MESH)

    loads = [
        pltpu.make_async_copy(source, target, load.at[i])
        for i, (source, target) in enumerate((
            (ctx_hbm.at[0], b_ctx), (item_hbm.at[0], b_item), (user_hbm.at[0], b_user), (count_hbm, b_count),
            (values_hbm.at[0, 0], values), (rows_hbm, fac.at[0]), (core_hbm, core), (slab_hbm, slab),
        ))
    ]
    for copy in loads:
        copy.start()
    pl.semaphore_wait(barrier, n_user + n_item - 2)
    fac_copies = []
    for d in range(1, n_user):
        copy = pltpu.make_async_remote_copy(
            src_ref=rows_hbm, dst_ref=fac.at[d], send_sem=fac_send.at[d], recv_sem=fac_recv.at[d],
            device_id={"user": lax.rem(me_u + d, n_user)}, device_id_type=MESH,
        )
        copy.start()
        fac_copies.append(copy)
    for copy in loads:
        copy.wait()

    ids = b_item[...]
    parts = [jnp.broadcast_to(r.astype(F32), (128, slots)) for r in (b_ctx[...], ids >> 7, ids & 127)]
    eye = (iota((slots, slots), 0) == iota((slots, slots), 1)).astype(F32).astype(BF16)
    columns = lax.dot_general(eye, jnp.concatenate(parts, axis=0).astype(BF16), NT, preferred_element_type=F32)
    start_col = columns[:, :128].astype(jnp.int32)
    item_col = (columns[:, 128:256] * 128.0 + columns[:, 256:384]).astype(jnp.int32)
    starts[...] = start_col

    turned = values[...].astype(F32)
    for bit in range(bw.bit_length() - 1):
        turned = jnp.where(((start_col >> bit) & 1) == 1, pltpu.roll(turned, 1 << bit, 1), turned)
    rf[pl.ds(rank * pitch, slots), :] = turned
    rf[pl.ds((rank + 1) * pitch, slots), :] = jnp.zeros((slots, bw), F32)

    cores = core[...].astype(F32)
    mixing = jnp.concatenate([cores[a] for a in range(rank)], axis=1).astype(BF16)
    for c in range(4):
        pieces = [jnp.zeros(slab.shape, BF16)] * 4
        pieces[c] = slab[...]
        bt[c] = jnp.concatenate(pieces, axis=0)
    live = iota((U_SH, slots), 1) < b_count[...]
    onehot = jnp.where((iota((U_SH, slots), 0) == b_user[...]) & live, 1.0, 0.0).astype(BF16)

    wanted = jnp.concatenate([item_col] * (rows // 128), axis=1)
    lane = iota((slots, rows), 1)
    chosen = jnp.zeros((slots, rank), F32)
    for d in range(n_user):
        held = lax.rem(me_u + n_user - d, n_user) * rows
        picks = jnp.where(lane + held == wanted, 1.0, 0.0).astype(BF16)
        if d:
            fac_copies[d - 1].wait()
        chosen = chosen + lax.dot_general(picks, fac[d], NT, preferred_element_type=F32)
    proj = jnp.dot(chosen.astype(BF16), mixing, preferred_element_type=F32).astype(BF16)
    for j in range(packs):
        yb[j] = proj[:, 128 * j : 128 * (j + 1)]

    half = slots // 2
    sub, ln = iota((8, 128), 0), iota((8, 128), 1)
    upper, same = sub < 4, (ln >> 5) == (sub & 3)

    def feature(begin, a):
        first = iota((half, bw), 1) >= starts[pl.ds(begin, half), :]
        full = jnp.dot(yb[a // 4, pl.ds(begin, half), :], bt[a % 4], preferred_element_type=F32)
        rf[pl.ds(a * pitch + begin, half), :] = jnp.where(first, full[:, :bw], full[:, bw:])

    def gram(base):
        left = jnp.concatenate([rf[pl.ds(a * pitch + base, 8), :] for a in range(rank + 2)], axis=0).astype(BF16)
        right = jnp.concatenate([rf[pl.ds(base + s, rank, stride=pitch), :] for s in range(8)], axis=0).astype(BF16)
        full = lax.dot_general(left, right, NT, preferred_element_type=F32)
        for a in range(rank + 1):
            part = full[8 * a : 8 * a + 8]
            gb[pl.ds(a * slots + base, 8), :] = jnp.where(same, jnp.where(upper, part[:, :128], part[:, 128:]), 0.0)

    groups = half // 8
    each = rank // groups
    for a in range(rank):
        feature(0, a)
    for g in range(groups):
        for a in range(each * g, each * (g + 1)):
            feature(half, a)
        gram(8 * g)
    for g in range(groups):
        gram(half + 8 * g)

    def summed(a):
        x = gb[pl.ds(a * slots, slots), :]
        high = x.astype(BF16)
        rest = (x - high.astype(F32)).astype(BF16)
        both = jnp.dot(onehot, jnp.concatenate([high, rest], axis=1), preferred_element_type=F32)
        return both[:, :128] + both[:, 128:]

    if per < 8:
        pay[...] = jnp.zeros(pay.shape, F32)

    def put(j, x):
        for q in range(n_item):
            pay[q, j, 0:per, :] = x[q * per : (q + 1) * per]

    blk = iota((U_SH, 128), 1) >> 5
    low, mid, even = blk < 2, (blk == 1) | (blk == 2), (blk & 1) == 0
    pay_copies = []
    bounds = [0, 4, 7, packs + 1]
    for part, (begin, end) in enumerate(zip(bounds[:-1], bounds[1:])):
        for j in range(begin, end):
            if j:
                x, w, y, v = (summed(4 * j - 4 + c) for c in range(4))
                one = jnp.where(low, x, y) + pltpu.roll(jnp.where(low, y, x), 64, 1)
                two = jnp.where(mid, w, v) + pltpu.roll(jnp.where(mid, v, w), 64, 1)
                put(j, jnp.where(even, one, two) + pltpu.roll(jnp.where(even, two, one), 96, 1))
            else:
                aim = summed(rank)
                aim = aim + pltpu.roll(aim, 64, 1)
                put(j, aim + pltpu.roll(aim, 32, 1))
        for d in range(1, n_item):
            to = lax.rem(me_i + d, n_item)
            copy = pltpu.make_async_remote_copy(
                src_ref=pay.at[to, begin:end], dst_ref=recv.at[d, begin:end],
                send_sem=pay_send.at[part, d], recv_sem=pay_recv.at[part, d],
                device_id={"item": to}, device_id_type=MESH,
            )
            copy.start()
            pay_copies.append(copy)
    for copy in pay_copies:
        copy.wait()
    total = pay[me_i]
    for d in range(1, n_item):
        total = total + recv[d]
    answer = solve([total[j + 1] for j in range(packs)], total[0])

    xg[me_i] = answer
    x_copies = []
    for d in range(1, n_item):
        copy = pltpu.make_async_remote_copy(
            src_ref=xg.at[me_i], dst_ref=xg.at[me_i], send_sem=x_send.at[d], recv_sem=x_recv.at[d],
            device_id={"item": lax.rem(me_i + d, n_item)}, device_id_type=MESH,
        )
        copy.start()
        x_copies.append(copy)
    for d in range(1, n_item):
        x_copies[d - 1].wait_send()
        source = lax.rem(me_i + n_item - d, n_item)
        pltpu.make_async_remote_copy(
            src_ref=xg.at[source], dst_ref=xg.at[source], send_sem=x_send.at[d], recv_sem=x_recv.at[d],
            device_id={"item": lax.rem(me_i + d, n_item)}, device_id_type=MESH,
        ).wait_recv()
    solved = jnp.concatenate([xg[q, 0:per, :] for q in range(n_item)] + [jnp.zeros((128 - U_SH, 128), F32)], axis=0)
    out[...] = jnp.transpose(solved)[:rank, :U_SH]


def solution(mesh):
    n_user, n_item = mesh.shape["user"], mesh.shape["item"]
    placed = (
        P("user", "item", None, None),
        P("user", "item", None),
        P("user", "item", None),
        P("user", "item", None),
        P("user", "item"),
        P(),
        P(("item", "user"), None),
        P(),
    )

    def local(values, block_user, block_item, block_ctx, block_count, core, item_factor, ctx_factor):
        rank = core.shape[0]
        slots, bw = values.shape[2], values.shape[3]
        packs = rank // 4
        solved = pl.pallas_call(
            functools.partial(kernel, n_user, n_item),
            out_shape=pltpu.VMEM((rank, U_SH), F32),
            in_specs=[pl.BlockSpec(memory_space=pltpu.HBM)] * 8,
            out_specs=pl.BlockSpec(memory_space=pltpu.VMEM),
            scratch_shapes=[
                pltpu.VMEM((slots, bw), BF16),
                pltpu.VMEM((1, slots), jnp.int32),
                pltpu.VMEM((1, slots), jnp.int32),
                pltpu.VMEM((1, slots), jnp.int32),
                pltpu.VMEM((1, 1), jnp.int32),
                pltpu.VMEM(core.shape, BF16),
                pltpu.VMEM((rank, ctx_factor.shape[0]), BF16),
                pltpu.VMEM((n_user, rank, item_factor.shape[0]), BF16),
                pltpu.VMEM((slots, 128), jnp.int32),
                pltpu.VMEM((4, 128, ctx_factor.shape[0]), BF16),
                pltpu.VMEM((packs, slots, 128), BF16),
                pltpu.VMEM(((rank + 2) * (slots + 8), bw), F32),
                pltpu.VMEM(((rank + 1) * slots, 128), F32),
                pltpu.VMEM((n_item, packs + 1, 8, 128), F32),
                pltpu.VMEM((n_item, packs + 1, 8, 128), F32),
                pltpu.VMEM((n_item, 8, 128), F32),
                pltpu.SemaphoreType.DMA((8,)),
                pltpu.SemaphoreType.DMA((n_user,)),
                pltpu.SemaphoreType.DMA((n_user,)),
                pltpu.SemaphoreType.DMA((3, n_item)),
                pltpu.SemaphoreType.DMA((3, n_item)),
                pltpu.SemaphoreType.DMA((n_item,)),
                pltpu.SemaphoreType.DMA((n_item,)),
            ],
            compiler_params=pltpu.CompilerParams(
                collective_id=0, has_side_effects=True, vmem_limit_bytes=48 * 1024 * 1024
            ),
        )(
            *(in_hbm(x) for x in (values, block_user, block_item, block_ctx)), block_count,
            *(in_hbm(x) for x in (core, jnp.transpose(item_factor), jnp.transpose(ctx_factor))),
        )
        return jnp.transpose(solved)

    return jax.shard_map(local, mesh=mesh, in_specs=placed, out_specs=P("user", None), check_vma=False)
```
